32 devices in a mesh: ctx: 8 (over z, y), exp: 4 (over x, core).
Axes of the slice: x: 2, y: 2, z: 4, core: 2. Of those that a mesh axis runs over, the one named last changes fastest.
Arguments:
- queries: bfloat16 [1024, 16, 576], P('ctx', 'exp'), may hold values from -300 to 300
- latents: bfloat16 [1024, 576], P('ctx'), may hold values from -6 to 6
- value_up: bfloat16 [16, 512, 128], P('exp'), may hold values from -0.5 to 0.5
- out_weight: bfloat16 [2048, 7168], P('exp', 'ctx'), may hold values from -0.25 to 0.25
Outputs:
- attn_out: bfloat16 [1024, 7168], P(('ctx', 'exp'))
The draws below stay inside these ranges and needn't reach their ends.
All inputs are finite; a program needn't handle non-finite values.
Results may differ from the reference program's by a relative error of at most 0.014.
Values may be sent and summed in bfloat16 or wider, within the bound.
No kernel may reach another device: no remote copies, remote signals or barrier semaphores. Data moves between devices by JAX's collectives and lax.ppermute only.
A program may use at most 64 MiB of HBM per device.

```python
import jax
import jax.numpy as jnp
from jax import lax

D = 7168
LAT = 576
VLAT = 512
VD = 128
HEADS = 16
TOKENS = 1024


def shared_fields(key):
    base = jax.random.fold_in(key, 11)
    key_a, key_b = jax.random.split(base, 2)
    latent_rows = jnp.clip(jax.random.normal(key_a, (TOKENS, LAT), jnp.float32), -6.0, 6.0)
    query_rows = jnp.clip(jax.random.normal(key_b, (TOKENS, HEADS, LAT), jnp.float32), -6.0, 6.0)
    return (query_rows, latent_rows)


def draw_queries(key, part):
    query_rows, latent_rows = shared_fields(key)
    return query_rows.astype(jnp.bfloat16)


def draw_latents(key, part):
    query_rows, latent_rows = shared_fields(key)
    return latent_rows.astype(jnp.bfloat16)


def level_of(own_key, shape, cuts, smallest, high):
    def one(dim, shards_of):
        draws = jax.random.uniform(jax.random.fold_in(jax.random.fold_in(own_key, 6), dim), (shards_of,), jnp.float32, smallest / len(cuts), high / len(cuts))
        return jnp.repeat(jnp.exp(draws), shape[dim] // shards_of).reshape((-1,) + (1,) * (len(shape) - dim - 1))

    factor_of = one(*cuts[0])
    for cut in cuts[1:]:
        factor_of = factor_of * one(*cut)
    return factor_of


def scatter_about(key, dims, spread, limit, cuts=(), dtype=jnp.bfloat16):
    entries = spread * jax.random.normal(key, dims, jnp.float32)
    if cuts:
        entries = entries * level_of(key, dims, cuts, -0.22, 0.18)
    return jnp.clip(entries, -limit, limit).astype(dtype)


def setup_inputs(seed: int = 0) -> dict:
    key_of = jax.random.split(jax.random.key(seed), 5)
    return {
        "queries": draw_queries(jax.random.fold_in(key_of[4], 71), 0),
        "latents": draw_latents(jax.random.fold_in(key_of[4], 71), 0),
        "value_up": scatter_about(key_of[2], (HEADS, VLAT, VD), (VLAT // 4) ** -0.5, 0.5, ((0, 4),)),
        "out_weight": scatter_about(key_of[3], (HEADS * VD, D), (HEADS * VD // 4) ** -0.5, 0.25, ((0, 4), (1, 8))),
    }


score_scale = 192.0 ** -0.5


def reference(queries, latents, value_up, out_weight):
    position = jnp.arange(TOKENS)
    visible = position[None, :] <= position[:, None]
    value_part = latents[:, :VLAT]

    def one_head(pair):
        head_query, head_up = pair
        scores = jnp.dot(head_query, latents.T, preferred_element_type=jnp.float32) * score_scale
        scores = jnp.where(visible, scores, -jnp.inf)
        top = jnp.max(scores, axis=1, keepdims=True)
        expo = jnp.where(visible, jnp.exp(scores - top), 0.0)
        total = jnp.sum(expo, axis=1, keepdims=True)
        weights = expo.astype(jnp.bfloat16)
        context = (jnp.dot(weights, value_part, preferred_element_type=jnp.float32) / total).astype(jnp.bfloat16)
        return jnp.dot(context, head_up, preferred_element_type=jnp.float32).astype(jnp.bfloat16)

    per_head = lax.map(one_head, (jnp.moveaxis(queries, 1, 0), value_up))
    values = jnp.moveaxis(per_head, 0, 1).reshape(TOKENS, HEADS * VD)
    return jnp.dot(values, out_weight, preferred_element_type=jnp.float32).astype(jnp.bfloat16)
```

```python
import jax
import jax.numpy as jnp
from jax import lax
from jax.sharding import PartitionSpec as P

VLAT = 512

score_scale = 192.0 ** (-0.5)


def send(value, axis, size, shift):
    return lax.ppermute(value, axis, [(i, i ^ shift) for i in range(size)])


def gather_latents(latents, ctx, exp, core):
    count, heads = lax.axis_size("ctx"), lax.axis_size("exp")

    def fetch(piece, shifts):
        pairs = [
            (c * heads + e, (c ^ shifts[e % 2]) * heads + e) for c in range(count) for e in range(heads)
        ]
        return lax.ppermute(piece, ("ctx", "exp"), pairs)

    blocks, owners = [latents], [ctx]
    half = latents.shape[0] // 2
    for low in range(count - 2, 1, -2):
        shifts = (low - (low % 2), low - (low % 2) + 1)
        mine = fetch(latents, shifts)
        blocks += [mine, send(mine, "exp", heads, 1)]
        owners += [ctx ^ jnp.where(core == 0, shifts[0], shifts[1]), ctx ^ jnp.where(core == 0, shifts[1], shifts[0])]
    mine = fetch(lax.dynamic_slice_in_dim(latents, core * half, half, 0), (1, 1))
    blocks += [mine, send(mine, "exp", heads, 1)]
    owners += [ctx ^ 1, ctx ^ 1]
    return blocks, owners


def gather_weight(out_weight, count, heads):
    half = out_weight.shape[0] // 2
    beside = send(out_weight, "ctx", count, 1)
    near = [(out_weight, beside)]
    for shift in range(2, heads, 2):
        across = send(out_weight, "exp", heads, shift)
        upper = send(beside[:half], "exp", heads, shift)
        lower = send(across[half:], "ctx", count, 1)
        near.append((across, jnp.concatenate([upper, lower], 0)))
    rows = []
    for pair in near:
        rows.append(jnp.concatenate(pair, 1))
        rows.append(jnp.concatenate([send(p, "exp", heads, 1) for p in pair], 1))
    return jnp.concatenate(rows, 0)


def shards(queries, latents, value_up, out_weight):
    count, heads = lax.axis_size("ctx"), lax.axis_size("exp")
    ctx, exp = lax.axis_index("ctx"), lax.axis_index("exp")
    core = exp % 2
    tokens, own_heads, _ = queries.shape
    part = tokens // heads
    width = out_weight.shape[1]

    keys, owners = gather_latents(latents, ctx, exp, core)
    weight = gather_weight(out_weight, count, heads)

    order = exp ^ jnp.arange(heads)
    rows = jnp.take(queries.reshape(heads, part, own_heads, -1), order, axis=0)
    rows = rows.reshape(tokens, own_heads, -1).transpose(1, 0, 2)
    row_pos = ctx * tokens + (order[:, None] * part + jnp.arange(part)[None, :]).reshape(-1)
    key_pos = jnp.concatenate(
        [owner * tokens + jnp.arange(k.shape[0]) for owner, k in zip(owners[:-2], keys[:-2])]
        + [owner * tokens + jnp.zeros(k.shape[0], jnp.int32) for owner, k in zip(owners[-2:], keys[-2:])]
    )
    key = jnp.concatenate(keys, 0)
    visible = (key_pos[None, :] <= row_pos[:, None])[None]
    scores = jnp.einsum("htd,sd->hts", rows, key, preferred_element_type=jnp.float32) * score_scale
    scores = jnp.where(visible, scores, -1e30)
    expo = jnp.where(visible, jnp.exp(scores - jnp.max(scores, axis=2, keepdims=True)), 0.0)
    total = jnp.sum(expo, axis=2, keepdims=True)
    context = jnp.einsum(
        "hts,sc->htc", expo.astype(jnp.bfloat16), key[:, :VLAT], preferred_element_type=jnp.float32
    )
    context = (context / total).astype(jnp.bfloat16)
    values = jnp.einsum("htc,hcd->thd", context, value_up, preferred_element_type=jnp.float32).astype(jnp.bfloat16)
    values = values.reshape(heads // 2, 2, part, -1)

    held = [values[0]] + [send(values[s // 2], "exp", heads, s) for s in range(2, heads, 2)]
    held = jnp.stack(held)
    other = send(held[:, 1], "exp", heads, 1)
    full = jnp.stack([held[:, 0], other], 1).reshape(heads, part, -1).transpose(1, 0, 2).reshape(part, -1)

    gathered = [full] + [send(full, "ctx", count, s) for s in range(2, count, 2)]
    gathered = jnp.concatenate(gathered, 0)
    result = jnp.dot(gathered, weight, preferred_element_type=jnp.float32).astype(jnp.bfloat16)
    result = result.reshape(count // 2, part, -1)
    final = jnp.zeros((part, count * width), jnp.bfloat16)
    for s in range(0, count, 2):
        block = result[s // 2]
        if s:
            block = send(block, "ctx", count, s)
        for side in range(2):
            final = lax.dynamic_update_slice(
                final, block[:, side * width : (side + 1) * width], (0, (ctx ^ (s + side)) * width)
            )
    return final


def solution(mesh):
    in_specs = (P("ctx", "exp", None), P("ctx", None), P("exp", None, None), P("exp", "ctx"))
    out_specs = P(("ctx", "exp"), None)
    return jax.shard_map(shards, mesh=mesh, in_specs=in_specs, out_specs=out_specs, check_vma=False)
```

```python
import functools

import jax
import jax.numpy as jnp
from jax import lax
from jax.experimental import pallas as pl
from jax.experimental.pallas import tpu as pltpu
from jax.sharding import PartitionSpec as P

VLAT = 512

score_scale = 192.0 ** (-0.5)

VMEM = pl.BlockSpec(memory_space=pltpu.VMEM)
SMEM = pl.BlockSpec(memory_space=pltpu.SMEM)


def send(value, axis, size, shift):
    return lax.ppermute(value, axis, [(i, i ^ shift) for i in range(size)])


def after(value, *others):
    return lax.optimization_barrier((value, *others))[0]


def gather_latents(own, ctx, core, count, heads):
    def fetch(shifts):
        pairs = [
            (c * heads + e, (c ^ shifts[e % 2]) * heads + e) for c in range(count) for e in range(heads)
        ]
        return lax.ppermute(own, ("ctx", "exp"), pairs)

    shifts = [(low, low + 1) for low in range(count - 2, 1, -2)]
    mine = [fetch(pair) for pair in shifts]
    beside = fetch((1, 1))
    other = [send(block, "exp", heads, 1) for block in mine]
    blocks, owners = [own], [ctx]
    for (even, odd), a, b in zip(shifts, mine, other):
        blocks += [a, b]
        owners += [ctx ^ jnp.where(core == 0, even, odd), ctx ^ jnp.where(core == 0, odd, even)]
    return blocks + [beside], owners + [ctx ^ 1]


def attend(part, place, query, *refs):
    *blocks, value_up, values, keys = refs
    own_heads, tokens, _ = query.shape
    width = blocks[0].shape[1]
    count = len(blocks)
    for j, block in enumerate(blocks):
        keys[:, j * width : (j + 1) * width] = block[...]
    ctx, exp = place[count], place[count + 1]
    row = lax.broadcasted_iota(jnp.int32, (tokens, width), 0)
    row = ((row // part) ^ exp) * part + row % part
    col = lax.broadcasted_iota(jnp.int32, (tokens, width), 1)
    inside = col <= row
    group = 2
    for first in range(0, own_heads, group):
        rows = query[first : first + group].reshape(group * tokens, -1)
        scores = jnp.dot(rows, keys[...], preferred_element_type=jnp.float32) * score_scale
        pieces = [
            jnp.where(jnp.concatenate([inside] * group, 0), scores[:, :width], -1e30)
        ]
        for j in range(1, count):
            pieces.append(jnp.where(place[j] < ctx, scores[:, j * width : (j + 1) * width], -1e30))
        scores = jnp.concatenate(pieces, 1)
        expo = jnp.exp(scores - jnp.max(scores, axis=1, keepdims=True))
        total = jnp.sum(expo, axis=1, keepdims=True)
        context = lax.dot_general(
            expo.astype(jnp.bfloat16),
            keys[:VLAT],
            (((1,), (1,)), ((), ())),
            preferred_element_type=jnp.float32,
        )
        context = (context / total).astype(jnp.bfloat16)
        for h in range(group):
            up = jnp.dot(
                context[h * tokens : (h + 1) * tokens], value_up[first + h], preferred_element_type=jnp.float32
            )
            depth = value_up.shape[2]
            values[:, (first + h) * depth : (first + h + 1) * depth] = up.astype(values.dtype)


def project(splits, values, *refs):
    *pieces, keep, away = refs
    half = values.shape[0] // 2
    width = pieces[0].shape[1]
    at = 0
    for group, size in enumerate(splits):
        total, depth = None, 0
        for piece in pieces[at : at + size]:
            term = jnp.dot(
                values[:, depth : depth + piece.shape[0]], piece[...], preferred_element_type=jnp.float32
            )
            total = term if total is None else total + term
            depth += piece.shape[0]
        at += size
        keep[:, group * width : (group + 1) * width] = total[:half]
        away[:, group * width : (group + 1) * width] = total[half:].astype(away.dtype)


def shards(queries, latents, value_up, out_weight):
    count, heads = lax.axis_size("ctx"), lax.axis_size("exp")
    ctx, exp = lax.axis_index("ctx"), lax.axis_index("exp")
    core = exp % 2
    tokens, own_heads, lat = queries.shape
    part = tokens // heads
    width = out_weight.shape[1]
    inner = own_heads * value_up.shape[2]
    half = inner // 2

    across = [send(out_weight, "exp", heads, s) for s in range(2, heads, 2)]
    blocks, owners = gather_latents(latents.T, ctx, core, count, heads)
    beside = send(after(out_weight, *blocks[1::2]), "ctx", count, 1)
    upper = [send(beside[:half], "exp", heads, s) for s in range(2, heads, 2)]
    lower = [send(a[half:], "ctx", count, 1) for a in across]

    order = exp ^ jnp.arange(heads)
    rows = jnp.take(queries.reshape(heads, part, own_heads, lat), order, axis=0)
    rows = rows.reshape(tokens, own_heads, lat).transpose(1, 0, 2)
    place = jnp.stack(owners + [ctx, exp]).astype(jnp.int32)
    values = pl.pallas_call(
        functools.partial(attend, part),
        out_shape=jax.ShapeDtypeStruct((tokens, inner), jnp.bfloat16),
        in_specs=[SMEM] + [VMEM] * (len(blocks) + 2),
        out_specs=VMEM,
        scratch_shapes=[pltpu.VMEM((lat, count * tokens), jnp.bfloat16)],
        compiler_params=pltpu.CompilerParams(vmem_limit_bytes=48 * 2**20),
        cost_estimate=pl.CostEstimate(
            flops=2 * tokens * own_heads * count * tokens * (lat + VLAT),
            bytes_accessed=2 * (rows.size + value_up.size + count * latents.size),
            transcendentals=tokens * own_heads * count * tokens,
        ),
    )(place, rows, *blocks, value_up)

    values = values.reshape(heads // 2, 2 * part, inner)
    held = [values[0]] + [send(values[s // 2], "exp", heads, s) for s in range(2, heads, 2)]
    held = jnp.concatenate(held, 1)
    gathered = [held] + [send(held, "ctx", count, s) for s in range(2, count, 2)]
    gathered = jnp.concatenate([g[:part] for g in gathered] + [g[part:] for g in gathered], 0)

    pieces, splits = [out_weight, *across], [len(across) + 1]
    pieces.append(beside)
    for u, l in zip(upper, lower):
        pieces += [u, l]
    splits.append(1 + 2 * len(across))
    mine = count // 2 * part
    keep, away = pl.pallas_call(
        functools.partial(project, splits),
        out_shape=(
            jax.ShapeDtypeStruct((mine, 2 * width), jnp.float32),
            jax.ShapeDtypeStruct((mine, 2 * width), jnp.bfloat16),
        ),
        in_specs=[VMEM] * (1 + len(pieces)),
        out_specs=(VMEM, VMEM),
        compiler_params=pltpu.CompilerParams(vmem_limit_bytes=48 * 2**20),
        cost_estimate=pl.CostEstimate(
            flops=2 * gathered.size * 2 * width,
            bytes_accessed=2 * (gathered.size + 2 * width * gathered.shape[1]) + 6 * mine * 2 * width,
            transcendentals=0,
        ),
    )(gathered, *pieces)
    result = (keep + send(away, "exp", heads, 1).astype(jnp.float32)).astype(jnp.bfloat16)
    result = result.reshape(count // 2, part, 2 * width)
    final = jnp.zeros((part, count * width), jnp.bfloat16)
    for s in range(0, count, 2):
        block = result[s // 2]
        if s:
            block = send(block, "ctx", count, s)
        for side in range(2):
            final = lax.dynamic_update_slice(
                final, block[:, side * width : (side + 1) * width], (0, (ctx ^ (s + side)) * width)
            )
    return final


def solution(mesh):
    in_specs = (P("ctx", "exp", None), P("ctx", None), P("exp", None, None), P("exp", "ctx"))
    out_specs = P(("ctx", "exp"), None)
    return jax.shard_map(shards, mesh=mesh, in_specs=in_specs, out_specs=out_specs, check_vma=False)
```

```python
import functools

import jax
import jax.numpy as jnp
from jax import lax
from jax.experimental import pallas as pl
from jax.experimental.pallas import tpu as pltpu
from jax.sharding import PartitionSpec as P

VLAT = 512

score_scale = 192.0 ** (-0.5)

VMEM = pl.BlockSpec(memory_space=pltpu.VMEM)
SMEM = pl.BlockSpec(memory_space=pltpu.SMEM)


def send(value, axis, size, shift):
    return lax.ppermute(value, axis, [(i, i ^ shift) for i in range(size)])


def after(value, *others):
    return lax.optimization_barrier((value, *others))[0]


def route(value, count, heads, shift):
    pairs = [
        (c * heads + e, (c ^ shift[e % 2][0]) * heads + (e ^ shift[e % 2][1]))
        for c in range(count)
        for e in range(heads)
    ]
    return lax.ppermute(value, ("ctx", "exp"), pairs)


def gather_latents(own, ctx, core, count, heads):
    shifts = [(low, low + 1) for low in range(count - 2, 1, -2)]
    mine = [route(own, count, heads, ((even, 0), (odd, 0))) for even, odd in shifts]
    beside = send(own, "ctx", count, 1)
    other = [send(block, "exp", heads, 1) for block in mine]
    blocks, owners = [own], [ctx]
    for (even, odd), a, b in zip(shifts, mine, other):
        blocks += [a, b]
        owners += [ctx ^ jnp.where(core == 0, even, odd), ctx ^ jnp.where(core == 0, odd, even)]
    return blocks + [beside], owners + [ctx ^ 1]


def attend(part, low, place, query, *refs):
    *blocks, value_up, values, keys = refs
    own_heads, tokens, _ = query.shape
    width = blocks[0].shape[1]
    count = len(blocks)
    for j, block in enumerate(blocks):
        keys[:, j * width : (j + 1) * width] = block[...]
    ctx, exp = place[count], place[count + 1]
    row = lax.broadcasted_iota(jnp.int32, (tokens, width), 0) + low
    row = ((row // part) ^ exp) * part + row % part
    col = lax.broadcasted_iota(jnp.int32, (tokens, width), 1)
    inside = col <= row
    group = own_heads
    for first in range(0, own_heads, group):
        rows = query[first : first + group].reshape(group * tokens, -1)
        scores = jnp.dot(rows, keys[...], preferred_element_type=jnp.float32) * score_scale
        pieces = [
            jnp.where(jnp.concatenate([inside] * group, 0), scores[:, :width], -1e30)
        ]
        for j in range(1, count):
            pieces.append(jnp.where(place[j] < ctx, scores[:, j * width : (j + 1) * width], -1e30))
        scores = jnp.concatenate(pieces, 1)
        expo = jnp.exp(scores - jnp.max(scores, axis=1, keepdims=True))
        total = jnp.sum(expo, axis=1, keepdims=True)
        context = lax.dot_general(
            expo.astype(jnp.bfloat16),
            keys[:VLAT],
            (((1,), (1,)), ((), ())),
            preferred_element_type=jnp.float32,
        )
        context = (context / total).astype(jnp.bfloat16)
        for h in range(group):
            up = jnp.dot(
                context[h * tokens : (h + 1) * tokens], value_up[first + h], preferred_element_type=jnp.float32
            )
            depth = value_up.shape[2]
            values[:, (first + h) * depth : (first + h + 1) * depth] = up.astype(values.dtype)


def project(place, values, own, first, second, corner, *refs):
    *rest, keep, away = refs
    half = values.shape[0] // 2
    depth, width = own.shape

    def columns(at, pieces):
        total = None
        for j, piece in enumerate(pieces):
            term = jnp.dot(
                values[:, j * depth : (j + 1) * depth], piece[...], preferred_element_type=jnp.float32
            )
            total = term if total is None else total + term
        keep[:, at : at + width] = total[:half]
        away[:, at : at + width] = total[half:].astype(away.dtype)

    def both(across, beside):
        columns(0, [own, across, *rest[::2]])
        columns(width, [beside, corner, *rest[1::2]])

    @pl.when(place[0] == 0)
    def _():
        both(first, second)

    @pl.when(place[0] != 0)
    def _():
        both(second, first)


def shards(queries, latents, value_up, out_weight):
    count, heads = lax.axis_size("ctx"), lax.axis_size("exp")
    ctx, exp = lax.axis_index("ctx"), lax.axis_index("exp")
    core = exp % 2
    tokens, own_heads, lat = queries.shape
    part = tokens // heads
    width = out_weight.shape[1]
    inner = own_heads * value_up.shape[2]

    first = route(out_weight, count, heads, ((0, 2), (1, 0)))
    blocks, owners = gather_latents(latents.T, ctx, core, count, heads)
    second = route(out_weight, count, heads, ((1, 0), (0, 2)))
    corner = route(first, count, heads, ((1, 0), (0, 2)))
    rest = []
    for s in range(4, heads, 2):
        rest += [send(out_weight, "exp", heads, s), route(out_weight, count, heads, ((1, s), (1, s)))]

    order = exp ^ jnp.arange(heads)
    rows = jnp.take(queries.reshape(heads, part, own_heads, lat), order, axis=0)
    rows = rows.reshape(tokens, own_heads, lat).transpose(1, 0, 2)
    rows = after(rows, first)
    place = jnp.stack(owners + [ctx, exp]).astype(jnp.int32)

    def attention(low, high):
        size = high - low
        return pl.pallas_call(
            functools.partial(attend, part, low),
            out_shape=jax.ShapeDtypeStruct((size, inner), jnp.bfloat16),
            in_specs=[SMEM] + [VMEM] * (len(blocks) + 2),
            out_specs=VMEM,
            scratch_shapes=[pltpu.VMEM((lat, count * tokens), jnp.bfloat16)],
            compiler_params=pltpu.CompilerParams(vmem_limit_bytes=48 * 2**20),
            cost_estimate=pl.CostEstimate(
                flops=2 * size * own_heads * count * tokens * (lat + VLAT),
                bytes_accessed=2 * (rows.size + value_up.size + count * latents.size),
                transcendentals=size * own_heads * count * tokens,
            ),
        )(place, rows[:, low:high], *blocks, value_up)

    away = attention(2 * part, tokens)
    away = [send(away[(s - 2) * part : s * part], "exp", heads, s) for s in range(2, heads, 2)]
    held = jnp.concatenate([attention(0, 2 * part)] + away, 1)
    held = after(held, second)
    gathered = [held] + [send(held, "ctx", count, s) for s in range(2, count, 2)]
    gathered = jnp.concatenate([g[:part] for g in gathered] + [g[part:] for g in gathered], 0)

    mine = count // 2 * part
    keep, away = pl.pallas_call(
        project,
        out_shape=(
            jax.ShapeDtypeStruct((mine, 2 * width), jnp.float32),
            jax.ShapeDtypeStruct((mine, 2 * width), jnp.bfloat16),
        ),
        in_specs=[SMEM] + [VMEM] * (5 + len(rest)),
        out_specs=(VMEM, VMEM),
        compiler_params=pltpu.CompilerParams(vmem_limit_bytes=48 * 2**20),
        cost_estimate=pl.CostEstimate(
            flops=2 * gathered.size * 2 * width,
            bytes_accessed=2 * (gathered.size + 2 * width * gathered.shape[1]) + 6 * mine * 2 * width,
            transcendentals=0,
        ),
    )(core[None].astype(jnp.int32), gathered, out_weight, first, second, corner, *rest)
    result = (keep + send(away, "exp", heads, 1).astype(jnp.float32)).astype(jnp.bfloat16)
    result = result.reshape(count // 2, part, 2 * width)
    final = jnp.zeros((part, count * width), jnp.bfloat16)
    for s in range(0, count, 2):
        block = result[s // 2]
        if s:
            block = send(block, "ctx", count, s)
        for side in range(2):
            final = lax.dynamic_update_slice(
                final, block[:, side * width : (side + 1) * width], (0, (ctx ^ (s + side)) * width)
            )
    return final


def solution(mesh):
    in_specs = (P("ctx", "exp", None), P("ctx", None), P("exp", None, None), P("exp", "ctx"))
    out_specs = P(("ctx", "exp"), None)
    return jax.shard_map(shards, mesh=mesh, in_specs=in_specs, out_specs=out_specs, check_vma=False)
```

```python
import functools

import jax
import jax.numpy as jnp
from jax import lax
from jax.experimental import pallas as pl
from jax.experimental.pallas import tpu as pltpu
from jax.sharding import PartitionSpec as P

VLAT = 512

score_scale = 192.0 ** (-0.5)

VMEM = pl.BlockSpec(memory_space=pltpu.VMEM)
SMEM = pl.BlockSpec(memory_space=pltpu.SMEM)


def send(value, axis, size, shift):
    return lax.ppermute(value, axis, [(i, i ^ shift) for i in range(size)])


def route(value, count, heads, shift):
    pairs = [
        (c * heads + e, (c ^ shift[e % 2][0]) * heads + (e ^ shift[e % 2][1]))
        for c in range(count)
        for e in range(heads)
    ]
    return lax.ppermute(value, ("ctx", "exp"), pairs)


def after(value, *others):
    return lax.optimization_barrier((value, *others))[0]


def gather_latents(own, ctx, core, count, heads):
    shifts = [(low, low + 1) for low in range(count - 2, 1, -2)]
    mine = [route(own, count, heads, ((even, 0), (odd, 0))) for even, odd in shifts]
    beside = send(own, "ctx", count, 1)
    other = [send(block, "exp", heads, 1) for block in mine]
    blocks, owners = [own], [ctx]
    for (even, odd), a, b in zip(shifts, mine, other):
        blocks += [a, b]
        owners += [ctx ^ jnp.where(core == 0, even, odd), ctx ^ jnp.where(core == 0, odd, even)]
    return blocks + [beside], owners + [ctx ^ 1]


def attend(part, low, place, query, *refs):
    *blocks, value_up, values, keys = refs
    own_heads, tokens, _ = query.shape
    width = blocks[0].shape[1]
    count = len(blocks)
    for j, block in enumerate(blocks):
        keys[:, j * width : (j + 1) * width] = block[...]
    ctx, exp = place[count], place[count + 1]
    row = lax.broadcasted_iota(jnp.int32, (tokens, width), 0) + low
    row = ((row // part) ^ exp) * part + row % part
    col = lax.broadcasted_iota(jnp.int32, (tokens, width), 1)
    inside = jnp.concatenate([col <= row] * own_heads, 0)
    scores = jnp.dot(
        query[...].reshape(own_heads * tokens, -1), keys[...], preferred_element_type=jnp.float32
    )
    scores = scores * score_scale
    pieces = [jnp.where(inside, scores[:, :width], -1e30)]
    for j in range(1, count):
        pieces.append(jnp.where(place[j] < ctx, scores[:, j * width : (j + 1) * width], -1e30))
    scores = jnp.concatenate(pieces, 1)
    expo = jnp.exp(scores - jnp.max(scores, axis=1, keepdims=True))
    total = jnp.sum(expo, axis=1, keepdims=True)
    context = lax.dot_general(
        expo.astype(jnp.bfloat16),
        keys[:VLAT],
        (((1,), (1,)), ((), ())),
        preferred_element_type=jnp.float32,
    )
    context = (context / total).astype(jnp.bfloat16)
    depth = value_up.shape[2]
    for h in range(own_heads):
        up = jnp.dot(
            context[h * tokens : (h + 1) * tokens], value_up[h], preferred_element_type=jnp.float32
        )
        values[:, h * depth : (h + 1) * depth] = up.astype(values.dtype)


def project(chips, groups, place, *refs):
    *operands, keep, away = refs
    values, pieces = operands[:chips], operands[chips:]
    rows, width = values[0].shape[0], pieces[0].shape[1]
    values = jnp.concatenate([part[...] for part in values], 0)

    def columns(at, depth, chosen):
        total = None
        for piece in chosen:
            term = jnp.dot(
                values[:, depth : depth + piece.shape[0]], piece[...], preferred_element_type=jnp.float32
            )
            total = term if total is None else total + term
            depth += piece.shape[0]
        total = total.reshape(chips, 2, rows // 2, width)
        keep[:, at : at + width] = total[:, 0].reshape(-1, width)
        away[:, at : at + width] = total[:, 1].reshape(-1, width).astype(away.dtype)

    for core in range(2):

        @pl.when(place[0] == core)
        def _():
            for j, (depth, *chosen) in enumerate(groups):
                columns(j * width, depth, [pieces[i] for i in chosen[core]])


def shards(queries, latents, value_up, out_weight):
    count, heads = lax.axis_size("ctx"), lax.axis_size("exp")
    ctx, exp = lax.axis_index("ctx"), lax.axis_index("exp")
    core = exp % 2
    tokens, own_heads, lat = queries.shape
    part = tokens // heads
    depth, width = out_weight.shape
    inner = own_heads * value_up.shape[2]

    blocks, owners = gather_latents(latents.T, ctx, core, count, heads)
    first = route(out_weight, count, heads, ((0, 2), (1, 0)))
    second = route(after(out_weight, blocks[-1]), count, heads, ((1, 0), (0, 2)))

    order = exp ^ jnp.arange(heads)
    rows = jnp.take(queries.reshape(heads, part, own_heads, lat), order, axis=0)
    rows = rows.reshape(tokens, own_heads, lat).transpose(1, 0, 2)
    place = jnp.stack(owners + [ctx, exp]).astype(jnp.int32)

    def attention(low, high):
        size = high - low
        return pl.pallas_call(
            functools.partial(attend, part, low),
            out_shape=jax.ShapeDtypeStruct((size, inner), jnp.bfloat16),
            in_specs=[SMEM] + [VMEM] * (len(blocks) + 2),
            out_specs=VMEM,
            scratch_shapes=[pltpu.VMEM((lat, count * tokens), jnp.bfloat16)],
            compiler_params=pltpu.CompilerParams(
                vmem_limit_bytes=count * tokens * (2 * lat + 32 * size * own_heads) + 2**22
            ),
            cost_estimate=pl.CostEstimate(
                flops=2 * size * own_heads * count * tokens * (lat + VLAT),
                bytes_accessed=2 * (rows.size + value_up.size + count * latents.size),
                transcendentals=size * own_heads * count * tokens,
            ),
        )(place, rows[:, low:high], *blocks, value_up)

    away = attention(2 * part, tokens)
    away = [send(away[(s - 2) * part : s * part], "exp", heads, s) for s in range(2, heads, 2)]
    kept = attention(0, 2 * part)
    held = jnp.concatenate([kept] + away, 1)
    corner = route(after(first, kept, *away), count, heads, ((1, 0), (0, 2)))
    values = [held] + [send(held, "ctx", count, s) for s in range(2, count, 2)]

    rest = []
    for s in range(4, heads, 2):
        rest += [send(out_weight, "exp", heads, s), route(out_weight, count, heads, ((1, s), (1, s)))]

    mine = len(values) * part

    def projection(groups, *pieces):
        out = (mine, len(groups) * width)
        return pl.pallas_call(
            functools.partial(project, len(values), groups),
            out_shape=(
                jax.ShapeDtypeStruct(out, jnp.float32),
                jax.ShapeDtypeStruct(out, jnp.bfloat16),
            ),
            in_specs=[SMEM] + [VMEM] * (len(values) + len(pieces)),
            out_specs=(VMEM, VMEM),
            compiler_params=pltpu.CompilerParams(vmem_limit_bytes=2**24),
            cost_estimate=pl.CostEstimate(
                flops=4 * mine * sum(p.size for p in pieces),
                bytes_accessed=2 * (len(values) * held.size + sum(p.size for p in pieces)) + 6 * mine * out[1],
                transcendentals=0,
            ),
        )(core[None].astype(jnp.int32), *values, *pieces)

    others = list(range(3, 3 + len(rest) // 2))
    keep, away = projection(
        [(0, [0, 1, *others], [0, 2, *others]), (0, [2], [1])], out_weight, first, second, *rest[::2]
    )
    other = send(away, "exp", heads, 1).astype(jnp.float32)
    last = list(range(1 + len(rest) // 2))
    keep_last, away = projection([(depth, last, last)], corner, *rest[1::2])
    other_last = send(away, "exp", heads, 1).astype(jnp.float32)
    left = keep[:, :width] + other[:, :width]
    right = keep[:, width:] + other[:, width:] + keep_last + other_last
    result = jnp.concatenate([left, right], 1).astype(jnp.bfloat16)
    result = result.reshape(count // 2, part, 2 * width)

    shifts = list(range(2, count, 2))
    if len(shifts) > 1:
        shifts = [shifts[1], shifts[0]] + shifts[2:]
    final = jnp.zeros((part, count * width), jnp.bfloat16)
    for s in [0] + shifts:
        block = send(result[s // 2], "ctx", count, s) if s else result[0]
        for side in range(2):
            final = lax.dynamic_update_slice(
                final, block[:, side * width : (side + 1) * width], (0, (ctx ^ (s + side)) * width)
            )
    return final


def solution(mesh):
    in_specs = (P("ctx", "exp", None), P("ctx", None), P("exp", None, None), P("exp", "ctx"))
    out_specs = P(("ctx", "exp"), None)
    return jax.shard_map(shards, mesh=mesh, in_specs=in_specs, out_specs=out_specs, check_vma=False)
```

```python
import functools

import jax
import jax.numpy as jnp
from jax import lax
from jax.experimental import pallas as pl
from jax.experimental.pallas import tpu as pltpu
from jax.sharding import PartitionSpec as P

VLAT = 512

score_scale = 192.0 ** (-0.5)

VMEM = pl.BlockSpec(memory_space=pltpu.VMEM)
SMEM = pl.BlockSpec(memory_space=pltpu.SMEM)


def send(value, axis, size, shift):
    return lax.ppermute(value, axis, [(i, i ^ shift) for i in range(size)])


def route(value, count, heads, shift):
    pairs = [
        (c * heads + e, (c ^ shift[e % 2][0]) * heads + (e ^ shift[e % 2][1]))
        for c in range(count)
        for e in range(heads)
    ]
    return lax.ppermute(value, ("ctx", "exp"), pairs)


def after(value, *others):
    return lax.optimization_barrier((value, *others))[0]


def gather_latents(own, ctx, core, count, heads):
    shifts = [(low, low + 1) for low in range(count - 2, 1, -2)]
    mine = [route(own, count, heads, ((even, 0), (odd, 0))) for even, odd in shifts]
    beside = send(own, "ctx", count, 1)
    other = [send(block, "exp", heads, 1) for block in mine]
    blocks, owners = [own], [ctx]
    for (even, odd), a, b in zip(shifts, mine, other):
        blocks += [a, b]
        owners += [ctx ^ jnp.where(core == 0, even, odd), ctx ^ jnp.where(core == 0, odd, even)]
    return blocks + [beside], owners + [ctx ^ 1]


def attend(part, low, place, query, *refs):
    *blocks, value_up, values, keys = refs
    own_heads, tokens, _ = query.shape
    width = blocks[0].shape[1]
    count = len(blocks)
    for j, block in enumerate(blocks):
        keys[:, j * width : (j + 1) * width] = block[...]
    ctx, exp = place[count], place[count + 1]
    row = lax.broadcasted_iota(jnp.int32, (tokens, width), 0) + low
    row = ((row // part) ^ exp) * part + row % part
    col = lax.broadcasted_iota(jnp.int32, (tokens, width), 1)
    inside = jnp.concatenate([col <= row] * own_heads, 0)
    scores = jnp.dot(
        query[...].reshape(own_heads * tokens, -1), keys[...], preferred_element_type=jnp.float32
    )
    scores = scores * score_scale
    pieces = [jnp.where(inside, scores[:, :width], -1e30)]
    for j in range(1, count):
        pieces.append(jnp.where(place[j] < ctx, scores[:, j * width : (j + 1) * width], -1e30))
    scores = jnp.concatenate(pieces, 1)
    expo = jnp.exp(scores - jnp.max(scores, axis=1, keepdims=True))
    total = jnp.sum(expo, axis=1, keepdims=True)
    context = lax.dot_general(
        expo.astype(jnp.bfloat16),
        keys[:VLAT],
        (((1,), (1,)), ((), ())),
        preferred_element_type=jnp.float32,
    )
    context = (context / total).astype(jnp.bfloat16)
    depth = value_up.shape[2]
    for h in range(own_heads):
        up = jnp.dot(
            context[h * tokens : (h + 1) * tokens], value_up[h], preferred_element_type=jnp.float32
        )
        values[:, h * depth : (h + 1) * depth] = up.astype(values.dtype)


def project(chips, groups, place, *refs):
    *operands, keep, away = refs
    values, pieces = operands[:chips], operands[chips:]
    rows, width = values[0].shape[0], pieces[0].shape[1]
    values = jnp.concatenate([part[...] for part in values], 0)

    def columns(at, depth, chosen):
        total = None
        for piece in chosen:
            term = jnp.dot(
                values[:, depth : depth + piece.shape[0]], piece[...], preferred_element_type=jnp.float32
            )
            total = term if total is None else total + term
            depth += piece.shape[0]
        total = total.reshape(chips, 2, rows // 2, width)
        keep[:, at : at + width] = total[:, 0].reshape(-1, width)
        away[:, at : at + width] = total[:, 1].reshape(-1, width).astype(away.dtype)

    for core in range(2):

        @pl.when(place[0] == core)
        def _():
            for j, (depth, *chosen) in enumerate(groups):
                columns(j * width, depth, [pieces[i] for i in chosen[core]])


def shards(queries, latents, value_up, out_weight):
    count, heads = lax.axis_size("ctx"), lax.axis_size("exp")
    ctx, exp = lax.axis_index("ctx"), lax.axis_index("exp")
    core = exp % 2
    tokens, own_heads, lat = queries.shape
    part = tokens // heads
    depth, width = out_weight.shape
    inner = own_heads * value_up.shape[2]

    blocks, owners = gather_latents(latents.T, ctx, core, count, heads)
    first = route(out_weight, count, heads, ((0, 2), (1, 0)))
    second = route(after(out_weight, blocks[-1]), count, heads, ((1, 0), (0, 2)))

    order = exp ^ jnp.arange(heads)
    rows = jnp.take(queries.reshape(heads, part, own_heads, lat), order, axis=0)
    rows = rows.reshape(tokens, own_heads, lat).transpose(1, 0, 2)
    place = jnp.stack(owners + [ctx, exp]).astype(jnp.int32)

    def attention(low, high):
        size = high - low
        return pl.pallas_call(
            functools.partial(attend, part, low),
            out_shape=jax.ShapeDtypeStruct((size, inner), jnp.bfloat16),
            in_specs=[SMEM] + [VMEM] * (len(blocks) + 2),
            out_specs=VMEM,
            scratch_shapes=[pltpu.VMEM((lat, count * tokens), jnp.bfloat16)],
            compiler_params=pltpu.CompilerParams(
                vmem_limit_bytes=count * tokens * (2 * lat + 32 * size * own_heads) + 2**22
            ),
            cost_estimate=pl.CostEstimate(
                flops=2 * size * own_heads * count * tokens * (lat + VLAT),
                bytes_accessed=2 * (rows.size + value_up.size + count * latents.size),
                transcendentals=size * own_heads * count * tokens,
            ),
        )(place, rows[:, low:high], *blocks, value_up)

    away = attention(2 * part, tokens)
    away = [send(away[(s - 2) * part : s * part], "exp", heads, s) for s in range(2, heads, 2)]
    kept = attention(0, 2 * part)
    held = jnp.concatenate([kept] + away, 1)
    corner = route(after(first, kept, *away), count, heads, ((1, 0), (0, 2)))
    values = [held] + [send(held, "ctx", count, s) for s in range(2, count, 2)]

    rest = []
    for s in range(4, heads, 2):
        rest += [send(out_weight, "exp", heads, s), route(out_weight, count, heads, ((1, s), (1, s)))]

    mine = len(values) * part

    def projection(groups, *pieces):
        out = (mine, len(groups) * width)
        return pl.pallas_call(
            functools.partial(project, len(values), groups),
            out_shape=(
                jax.ShapeDtypeStruct(out, jnp.float32),
                jax.ShapeDtypeStruct(out, jnp.bfloat16),
            ),
            in_specs=[SMEM] + [VMEM] * (len(values) + len(pieces)),
            out_specs=(VMEM, VMEM),
            compiler_params=pltpu.CompilerParams(vmem_limit_bytes=2**24),
            cost_estimate=pl.CostEstimate(
                flops=4 * mine * sum(p.size for p in pieces),
                bytes_accessed=2 * (len(values) * held.size + sum(p.size for p in pieces)) + 6 * mine * out[1],
                transcendentals=0,
            ),
        )(core[None].astype(jnp.int32), *values, *pieces)

    others = list(range(3, 3 + len(rest) // 2))
    keep, away = projection(
        [(0, [0, 1, *others], [0, 2, *others]), (0, [2], [1])], out_weight, first, second, *rest[::2]
    )
    other = send(away, "exp", heads, 1).astype(jnp.float32)
    last = list(range(1 + len(rest) // 2))
    keep_last, away = projection([(depth, last, last)], corner, *rest[1::2])
    other_last = send(away, "exp", heads, 1).astype(jnp.float32)
    here = keep[:, :width] + other[:, :width]
    beside = keep[:, width:] + other[:, width:] + keep_last + other_last
    left, right = jnp.where(ctx % 2 == 0, here, beside), jnp.where(ctx % 2 == 0, beside, here)
    result = jnp.concatenate([left, right], 1).astype(jnp.bfloat16)
    result = result.reshape(count // 2, part, 2 * width)

    shifts = list(range(2, count, 2))
    if len(shifts) > 1:
        shifts = [shifts[1], shifts[0]] + shifts[2:]
    final = jnp.zeros((part, count * width), jnp.bfloat16)
    for s in [0] + shifts:
        block = send(result[s // 2], "ctx", count, s) if s else result[0]
        final = lax.dynamic_update_slice(final, block, (0, (ctx ^ s) // 2 * 2 * width))
    return final


def solution(mesh):
    in_specs = (P("ctx", "exp", None), P("ctx", None), P("exp", None, None), P("exp", "ctx"))
    out_specs = P(("ctx", "exp"), None)
    return jax.shard_map(shards, mesh=mesh, in_specs=in_specs, out_specs=out_specs, check_vma=False)
```

```python
import functools

import jax
import jax.numpy as jnp
from jax import lax
from jax.experimental import pallas as pl
from jax.experimental.pallas import tpu as pltpu
from jax.sharding import PartitionSpec as P

VLAT = 512

score_scale = 192.0 ** (-0.5)

VMEM = pl.BlockSpec(memory_space=pltpu.VMEM)
SMEM = pl.BlockSpec(memory_space=pltpu.SMEM)


def send(value, axis, size, shift):
    return lax.ppermute(value, axis, [(i, i ^ shift) for i in range(size)])


def route(value, count, heads, shift):
    pairs = [
        (c * heads + e, (c ^ shift[e % 2][0]) * heads + (e ^ shift[e % 2][1]))
        for c in range(count)
        for e in range(heads)
    ]
    return lax.ppermute(value, ("ctx", "exp"), pairs)


def after(value, *others):
    return lax.optimization_barrier((value, *others))[0]


def gather_latents(own, ctx, core, count, heads):
    shifts = [(low, low + 1) for low in range(count - 2, 1, -2)]
    mine = [route(own, count, heads, ((even, 0), (odd, 0))) for even, odd in shifts]
    beside = send(own, "ctx", count, 1)
    other = [send(block, "exp", heads, 1) for block in mine]
    blocks, owners = [own], [ctx]
    for (even, odd), a, b in zip(shifts, mine, other):
        blocks += [a, b]
        owners += [ctx ^ jnp.where(core == 0, even, odd), ctx ^ jnp.where(core == 0, odd, even)]
    return blocks + [beside], owners + [ctx ^ 1]


def attend(part, low, place, query, *refs):
    *blocks, value_up, values, keys = refs
    own_heads, tokens, _ = query.shape
    width = blocks[0].shape[1]
    count = len(blocks)
    for j, block in enumerate(blocks):
        keys[:, j * width : (j + 1) * width] = block[...]
    ctx, exp = place[count], place[count + 1]
    row = lax.broadcasted_iota(jnp.int32, (tokens, width), 0) + low
    row = ((row // part) ^ exp) * part + row % part
    col = lax.broadcasted_iota(jnp.int32, (tokens, width), 1)
    inside = jnp.concatenate([col <= row] * own_heads, 0)
    scores = jnp.dot(
        query[...].reshape(own_heads * tokens, -1), keys[...], preferred_element_type=jnp.float32
    )
    scores = scores * score_scale
    pieces = [jnp.where(inside, scores[:, :width], -1e30)]
    for j in range(1, count):
        pieces.append(jnp.where(place[j] < ctx, scores[:, j * width : (j + 1) * width], -1e30))
    scores = jnp.concatenate(pieces, 1)
    expo = jnp.exp(scores - jnp.max(scores, axis=1, keepdims=True))
    total = jnp.sum(expo, axis=1, keepdims=True)
    context = lax.dot_general(
        expo.astype(jnp.bfloat16),
        keys[:VLAT],
        (((1,), (1,)), ((), ())),
        preferred_element_type=jnp.float32,
    )
    context = (context / total).astype(jnp.bfloat16)
    depth = value_up.shape[2]
    for h in range(own_heads):
        up = jnp.dot(
            context[h * tokens : (h + 1) * tokens], value_up[h], preferred_element_type=jnp.float32
        )
        values[:, h * depth : (h + 1) * depth] = up.astype(values.dtype)


def project(chips, groups, place, *refs):
    *operands, keep, away = refs
    values, pieces = operands[:chips], operands[chips:]
    rows, width = values[0].shape[0], pieces[0].shape[1]
    values = jnp.concatenate([part[...] for part in values], 0)

    def columns(at, depth, chosen):
        total = None
        for piece in chosen:
            term = jnp.dot(
                values[:, depth : depth + piece.shape[0]], piece[...], preferred_element_type=jnp.float32
            )
            total = term if total is None else total + term
            depth += piece.shape[0]
        total = total.reshape(chips, 2, rows // 2, width)
        keep[:, at : at + width] = total[:, 0].reshape(-1, width)
        away[:, at : at + width] = total[:, 1].reshape(-1, width).astype(away.dtype)

    for core in range(2):

        @pl.when(place[0] == core)
        def _():
            for j, (depth, *chosen) in enumerate(groups):
                columns(j * width, depth, [pieces[i] for i in chosen[core]])


def project_half(chips, depth, half, *refs):
    *operands, out = refs
    values, pieces = operands[:chips], operands[chips:]
    rows = values[0].shape[0]
    stop = depth + sum(piece.shape[0] for piece in pieces)
    chosen = [
        part[:, depth:stop].astype(jnp.float32)[half * rows // 2 : (half + 1) * rows // 2] for part in values
    ]
    chosen = jnp.concatenate(chosen, 0).astype(jnp.bfloat16)
    total, at = None, 0
    for piece in pieces:
        term = jnp.dot(
            chosen[:, at : at + piece.shape[0]], piece[...], preferred_element_type=jnp.float32
        )
        total = term if total is None else total + term
        at += piece.shape[0]
    out[...] = total.astype(out.dtype)


def shards(queries, latents, value_up, out_weight):
    count, heads = lax.axis_size("ctx"), lax.axis_size("exp")
    ctx, exp = lax.axis_index("ctx"), lax.axis_index("exp")
    core = exp % 2
    tokens, own_heads, lat = queries.shape
    part = tokens // heads
    depth, width = out_weight.shape
    inner = own_heads * value_up.shape[2]

    blocks, owners = gather_latents(latents.T, ctx, core, count, heads)
    first = route(out_weight, count, heads, ((0, 2), (1, 0)))
    second = route(after(out_weight, blocks[-1]), count, heads, ((1, 0), (0, 2)))

    order = exp ^ jnp.arange(heads)
    rows = jnp.take(queries.reshape(heads, part, own_heads, lat), order, axis=0)
    rows = rows.reshape(tokens, own_heads, lat).transpose(1, 0, 2)
    place = jnp.stack(owners + [ctx, exp]).astype(jnp.int32)

    def attention(low, high):
        size = high - low
        return pl.pallas_call(
            functools.partial(attend, part, low),
            out_shape=jax.ShapeDtypeStruct((size, inner), jnp.bfloat16),
            in_specs=[SMEM] + [VMEM] * (len(blocks) + 2),
            out_specs=VMEM,
            scratch_shapes=[pltpu.VMEM((lat, count * tokens), jnp.bfloat16)],
            compiler_params=pltpu.CompilerParams(
                vmem_limit_bytes=count * tokens * (2 * lat + 32 * size * own_heads) + 2**22
            ),
            cost_estimate=pl.CostEstimate(
                flops=2 * size * own_heads * count * tokens * (lat + VLAT),
                bytes_accessed=2 * (rows.size + value_up.size + count * latents.size),
                transcendentals=size * own_heads * count * tokens,
            ),
        )(place, rows[:, low:high], *blocks, value_up)

    away = attention(2 * part, tokens)
    away = [send(away[(s - 2) * part : s * part], "exp", heads, s) for s in range(2, heads, 2)]
    kept = attention(0, 2 * part)
    held = jnp.concatenate([kept] + away, 1)
    corner = route(after(first, kept, *away), count, heads, ((1, 0), (0, 2)))
    values = [held] + [send(held, "ctx", count, s) for s in range(2, count, 2)]

    rest = []
    for s in range(4, heads, 2):
        rest += [send(out_weight, "exp", heads, s), route(out_weight, count, heads, ((1, s), (1, s)))]

    mine = len(values) * part

    def projection(groups, *pieces):
        out = (mine, len(groups) * width)
        return pl.pallas_call(
            functools.partial(project, len(values), groups),
            out_shape=(
                jax.ShapeDtypeStruct(out, jnp.float32),
                jax.ShapeDtypeStruct(out, jnp.bfloat16),
            ),
            in_specs=[SMEM] + [VMEM] * (len(values) + len(pieces)),
            out_specs=(VMEM, VMEM),
            compiler_params=pltpu.CompilerParams(vmem_limit_bytes=2**24),
            cost_estimate=pl.CostEstimate(
                flops=4 * mine * sum(p.size for p in pieces),
                bytes_accessed=2 * (len(values) * held.size + sum(p.size for p in pieces)) + 6 * mine * out[1],
                transcendentals=0,
            ),
        )(core[None].astype(jnp.int32), *values, *pieces)

    others = list(range(3, 3 + len(rest) // 2))
    keep, away = projection(
        [(0, [0, 1, *others], [0, 2, *others]), (0, [2], [1])], out_weight, first, second, *rest[::2]
    )
    other = send(away, "exp", heads, 1).astype(jnp.float32)
    last = [corner, *rest[1::2]]

    def last_half(half, dtype):
        return pl.pallas_call(
            functools.partial(project_half, len(values), depth, half),
            out_shape=jax.ShapeDtypeStruct((mine, width), dtype),
            in_specs=[VMEM] * (len(values) + len(last)),
            out_specs=VMEM,
            compiler_params=pltpu.CompilerParams(vmem_limit_bytes=2**24),
            cost_estimate=pl.CostEstimate(
                flops=2 * mine * sum(p.size for p in last),
                bytes_accessed=2 * (len(values) * held.size + sum(p.size for p in last)) + 4 * mine * width,
                transcendentals=0,
            ),
        )(*values, *last)

    other_last = send(last_half(1, jnp.bfloat16), "exp", heads, 1).astype(jnp.float32)
    keep_last = last_half(0, jnp.float32)
    here = keep[:, :width] + other[:, :width]
    beside = keep[:, width:] + other[:, width:] + keep_last + other_last
    left, right = jnp.where(ctx % 2 == 0, here, beside), jnp.where(ctx % 2 == 0, beside, here)
    result = jnp.concatenate([left, right], 1).astype(jnp.bfloat16)
    result = result.reshape(count // 2, part, 2 * width)

    shifts = list(range(2, count, 2))
    if len(shifts) > 1:
        shifts = [shifts[1], shifts[0]] + shifts[2:]
    final = jnp.zeros((part, count * width), jnp.bfloat16)
    for s in [0] + shifts:
        block = send(result[s // 2], "ctx", count, s) if s else result[0]
        final = lax.dynamic_update_slice(final, block, (0, (ctx ^ s) // 2 * 2 * width))
    return final


def solution(mesh):
    in_specs = (P("ctx", "exp", None), P("ctx", None), P("exp", None, None), P("exp", "ctx"))
    out_specs = P(("ctx", "exp"), None)
    return jax.shard_map(shards, mesh=mesh, in_specs=in_specs, out_specs=out_specs, check_vma=False)
```

```python
import functools

import jax
import jax.numpy as jnp
from jax import lax
from jax.experimental import pallas as pl
from jax.experimental.pallas import tpu as pltpu
from jax.sharding import PartitionSpec as P

VLAT = 512

score_scale = 192.0 ** (-0.5)

VMEM = pl.BlockSpec(memory_space=pltpu.VMEM)
SMEM = pl.BlockSpec(memory_space=pltpu.SMEM)


def send(value, axis, size, shift):
    return lax.ppermute(value, axis, [(i, i ^ shift) for i in range(size)])


def route(value, count, heads, shift):
    pairs = [
        (c * heads + e, (c ^ shift[e % 2][0]) * heads + (e ^ shift[e % 2][1]))
        for c in range(count)
        for e in range(heads)
    ]
    return lax.ppermute(value, ("ctx", "exp"), pairs)


def after(value, *others):
    return lax.optimization_barrier((value, *others))[0]


def gather_latents(own, ctx, core, count, heads):
    shifts = [(low, low + 1) for low in range(count - 2, 1, -2)]
    mine = [route(own, count, heads, ((even, 0), (odd, 0))) for even, odd in shifts]
    beside = send(own, "ctx", count, 1)
    other = [send(block, "exp", heads, 1) for block in mine]
    blocks, owners = [own], [ctx]
    for (even, odd), a, b in zip(shifts, mine, other):
        blocks += [a, b]
        owners += [ctx ^ jnp.where(core == 0, even, odd), ctx ^ jnp.where(core == 0, odd, even)]
    return blocks + [beside], owners + [ctx ^ 1]


def attend(part, low, place, query, *refs):
    *blocks, value_up, values, keys = refs
    own_heads, tokens, _ = query.shape
    width = blocks[0].shape[1]
    count = len(blocks)
    for j, block in enumerate(blocks):
        keys[:, j * width : (j + 1) * width] = block[...]
    ctx, exp = place[count], place[count + 1]
    row = lax.broadcasted_iota(jnp.int32, (tokens, width), 0) + low
    row = ((row // part) ^ exp) * part + row % part
    col = lax.broadcasted_iota(jnp.int32, (tokens, width), 1)
    inside = jnp.concatenate([col <= row] * own_heads, 0)
    scores = jnp.dot(
        query[...].reshape(own_heads * tokens, -1), keys[...], preferred_element_type=jnp.float32
    )
    scores = scores * score_scale
    pieces = [jnp.where(inside, scores[:, :width], -1e30)]
    for j in range(1, count):
        pieces.append(jnp.where(place[j] < ctx, scores[:, j * width : (j + 1) * width], -1e30))
    scores = jnp.concatenate(pieces, 1)
    expo = jnp.exp(scores - jnp.max(scores, axis=1, keepdims=True))
    total = jnp.sum(expo, axis=1, keepdims=True)
    context = lax.dot_general(
        expo.astype(jnp.bfloat16),
        keys[:VLAT],
        (((1,), (1,)), ((), ())),
        preferred_element_type=jnp.float32,
    )
    context = (context / total).astype(jnp.bfloat16)
    depth = value_up.shape[2]
    for h in range(own_heads):
        up = jnp.dot(
            context[h * tokens : (h + 1) * tokens], value_up[h], preferred_element_type=jnp.float32
        )
        values[:, h * depth : (h + 1) * depth] = up.astype(values.dtype)


def project(chips, groups, place, *refs):
    *operands, keep, away = refs
    values, pieces = operands[:chips], operands[chips:]
    rows, width = values[0].shape[0], pieces[0].shape[1]
    values = jnp.concatenate([part[...] for part in values], 0)

    def columns(at, depth, chosen):
        total = None
        for piece in chosen:
            term = jnp.dot(
                values[:, depth : depth + piece.shape[0]], piece[...], preferred_element_type=jnp.float32
            )
            total = term if total is None else total + term
            depth += piece.shape[0]
        total = total.reshape(chips, 2, rows // 2, width)
        keep[:, at : at + width] = total[:, 0].reshape(-1, width)
        away[:, at : at + width] = total[:, 1].reshape(-1, width).astype(away.dtype)

    for core in range(2):

        @pl.when(place[0] == core)
        def _():
            for j, (depth, *chosen) in enumerate(groups):
                columns(j * width, depth, [pieces[i] for i in chosen[core]])


def shards(queries, latents, value_up, out_weight):
    count, heads = lax.axis_size("ctx"), lax.axis_size("exp")
    ctx, exp = lax.axis_index("ctx"), lax.axis_index("exp")
    core = exp % 2
    tokens, own_heads, lat = queries.shape
    part = tokens // heads
    depth, width = out_weight.shape
    inner = own_heads * value_up.shape[2]

    blocks, owners = gather_latents(latents.T, ctx, core, count, heads)
    first = route(out_weight, count, heads, ((0, 2), (1, 0)))
    second = route(after(out_weight, blocks[-1]), count, heads, ((1, 0), (0, 2)))

    order = exp ^ jnp.arange(heads)
    rows = jnp.take(queries.reshape(heads, part, own_heads, lat), order, axis=0)
    rows = rows.reshape(tokens, own_heads, lat).transpose(1, 0, 2)
    place = jnp.stack(owners + [ctx, exp]).astype(jnp.int32)

    def attention(low, high):
        size = high - low
        return pl.pallas_call(
            functools.partial(attend, part, low),
            out_shape=jax.ShapeDtypeStruct((size, inner), jnp.bfloat16),
            in_specs=[SMEM] + [VMEM] * (len(blocks) + 2),
            out_specs=VMEM,
            scratch_shapes=[pltpu.VMEM((lat, count * tokens), jnp.bfloat16)],
            compiler_params=pltpu.CompilerParams(
                vmem_limit_bytes=count * tokens * (2 * lat + 32 * size * own_heads) + 2**22
            ),
            cost_estimate=pl.CostEstimate(
                flops=2 * size * own_heads * count * tokens * (lat + VLAT),
                bytes_accessed=2 * (rows.size + value_up.size + count * latents.size),
                transcendentals=size * own_heads * count * tokens,
            ),
        )(place, rows[:, low:high], *blocks, value_up)

    away = attention(2 * part, tokens)
    away = [send(away[(s - 2) * part : s * part], "exp", heads, s) for s in range(2, heads, 2)]
    kept = attention(0, 2 * part)
    held = jnp.concatenate([kept] + away, 1)
    corner = route(after(first, kept, *away), count, heads, ((1, 0), (0, 2)))
    shifts = list(range(2, count, 2))
    if len(shifts) > 1:
        shifts = [shifts[1], shifts[0]] + shifts[2:]
    parts = {0: held, **{s: send(held, "ctx", count, s) for s in shifts}}
    values = [parts[s] for s in range(0, count, 2)]

    rest = []
    for s in range(4, heads, 2):
        rest += [send(out_weight, "exp", heads, s), route(out_weight, count, heads, ((1, s), (1, s)))]

    mine = len(values) * part

    def projection(groups, *pieces):
        out = (mine, len(groups) * width)
        return pl.pallas_call(
            functools.partial(project, len(values), groups),
            out_shape=(
                jax.ShapeDtypeStruct(out, jnp.float32),
                jax.ShapeDtypeStruct(out, jnp.bfloat16),
            ),
            in_specs=[SMEM] + [VMEM] * (len(values) + len(pieces)),
            out_specs=(VMEM, VMEM),
            compiler_params=pltpu.CompilerParams(vmem_limit_bytes=2**24),
            cost_estimate=pl.CostEstimate(
                flops=4 * mine * sum(p.size for p in pieces),
                bytes_accessed=2 * (len(values) * held.size + sum(p.size for p in pieces)) + 6 * mine * out[1],
                transcendentals=0,
            ),
        )(core[None].astype(jnp.int32), *values, *pieces)

    others = list(range(3, 3 + len(rest) // 2))
    keep, away = projection(
        [(0, [0, 1, *others], [0, 2, *others]), (0, [2], [1])], out_weight, first, second, *rest[::2]
    )
    other = send(away, "exp", heads, 1).astype(jnp.float32)
    last = list(range(1 + len(rest) // 2))
    keep_last, away = projection([(depth, last, last)], corner, *rest[1::2])
    other_last = send(away, "exp", heads, 1).astype(jnp.float32)
    here = keep[:, :width] + other[:, :width]
    beside = keep[:, width:] + other[:, width:] + keep_last + other_last
    left, right = jnp.where(ctx % 2 == 0, here, beside), jnp.where(ctx % 2 == 0, beside, here)
    result = jnp.concatenate([left, right], 1).astype(jnp.bfloat16)
    result = result.reshape(count // 2, part, 2 * width)

    final = jnp.zeros((part, count * width), jnp.bfloat16)
    for s in [0] + shifts:
        block = send(result[s // 2], "ctx", count, s) if s else result[0]
        final = lax.dynamic_update_slice(final, block, (0, (ctx ^ s) // 2 * 2 * width))
    return final


def solution(mesh):
    in_specs = (P("ctx", "exp", None), P("ctx", None), P("exp", None, None), P("exp", "ctx"))
    out_specs = P(("ctx", "exp"), None)
    return jax.shard_map(shards, mesh=mesh, in_specs=in_specs, out_specs=out_specs, check_vma=False)
```
